32 devices in a mesh: req: 8 (over z, y), grp: 4 (over x, core).
Axes of the slice: x: 2, y: 2, z: 4, core: 2. Of those that a mesh axis runs over, the one named last changes fastest.
Arguments:
- hidden: bfloat16 [8192, 1536], P(('req', 'grp')), may hold values from -48 to 48
- queries: bfloat16 [8192, 1536], P(('req', 'grp')), may hold values from -8 to 8
- new_cache: bfloat16 [8192, 256], P(('req', 'grp')), may hold values from -8 to 8
- cache_pool: bfloat16 [8192, 64, 256], P(('req', 'grp')), may hold values from -6 to 6
- cache_length: int32 [128], P(('req', 'grp')), may hold values from 1 to 4096
- page_table: int32 [128, 17], P(('req', 'grp')), may hold values from 0 to 95, as said below
- send_map: int32 [32, 96], P(('req', 'grp')), may hold values from 0 to 255, as said below
- out_weight: bfloat16 [1536, 1536], replicated, may hold values from -0.5 to 0.5
- norm_gain: bfloat16 [1536], replicated, may hold values from 0.099609375 to 1.8984375
- ffn_weight: bfloat16 [3, 1536, 4608], P(None, None, 'grp'), may hold values from -0.15625 to 0.15625
Outputs:
- block_out: bfloat16 [8192, 1536], P(('req', 'grp'))
The draws below stay inside these ranges and needn't reach their ends.
Inputs may be any that keep to these rules, and one draw needn't show every extreme that they name: `page_table`: the 68 entries of one device's requests are distinct; entry s * 3 + c names the page that device s sends to that device as its slot c. On every device all 3 slots of some source are named. `send_map`: entry d * 3 + c of row s is the slot of device s's pool that it sends to device d as slot c; the entries of a row are distinct.
All inputs are finite; a program needn't handle non-finite values.
Results may differ from the reference program's by a relative error of at most 0.012.
Values may be sent and summed in bfloat16 or wider, within the bound.
A program may use at most 128 MiB of HBM per device.

```python
import math
import jax
import jax.numpy as jnp
from jax import lax

D = 1536
HEADS = 12
HD = 128
FF = 4608
W = 1024
PAGE = 64
CACHE_MAX = 4096
POOL_DEV = 256
REQ_DEV = 4
NEW = 64
WPAGES = 17
CAP = 3
TOK_DEV = 256
REQUESTS = 128
TOKENS = 8192
DEVICES = 32


def pick_distinct(key, total, count, forced):
    first_key, second_key = jax.random.split(key)
    noise = jax.random.randint(first_key, (total,), 0, 1 << 20)
    index = jnp.arange(total, dtype=jnp.int32)
    ranking = jnp.where(forced, index, (noise + 1) * total + index)
    order = jnp.argsort(ranking, stable=True).astype(jnp.int32)
    chosen = order[:count]
    shuffle = jax.random.permutation(second_key, count)
    return chosen[shuffle]


def draw_page_table(key, part):
    total = DEVICES * CAP
    count = REQ_DEV * WPAGES

    def one_device(device_key):
        source_key, pick_key = jax.random.split(device_key)
        source = jax.random.randint(source_key, (), 0, DEVICES)
        slots = jnp.arange(total, dtype=jnp.int32)
        forced = (slots // CAP == source) | (slots == 0) | (slots == total - 1)
        return pick_distinct(pick_key, total, count, forced)
    tables = jax.vmap(one_device)(jax.random.split(jax.random.fold_in(key, 11), DEVICES))
    return tables.reshape(REQUESTS, WPAGES).astype(jnp.int32)


def draw_send_map(key, part):
    total = POOL_DEV
    count = DEVICES * CAP

    def one_device(device_key):
        values = jnp.arange(total, dtype=jnp.int32)
        forced = (values == 0) | (values == total - 1)
        return pick_distinct(device_key, total, count, forced)
    return jax.vmap(one_device)(jax.random.split(jax.random.fold_in(key, 23), DEVICES)).astype(jnp.int32)


def draw_hidden(key, part):
    row_key = jax.random.fold_in(key, 0)
    col_key = jax.random.fold_in(key, 1)
    base_key = jax.random.fold_in(key, 3)
    rows = jnp.exp(jax.random.uniform(row_key, (TOKENS, 1), jnp.float32, math.log(0.4), math.log(4.0)))
    cols = jnp.exp(jax.random.uniform(col_key, (1, D), jnp.float32, math.log(0.4), math.log(4.0)))
    base = jnp.clip(jax.random.normal(base_key, (TOKENS, D), jnp.float32), -3.0, 3.0)
    return (base * rows * cols).astype(jnp.bfloat16)


def draw_queries(key, part):
    width = HEADS * HD
    base = jnp.clip(2.0 * jax.random.normal(key, (TOKENS, width), jnp.float32), -8.0, 8.0)
    return base.astype(jnp.bfloat16)


def draw_new_cache(key, part):
    width = 2 * HD
    base = jnp.clip(jax.random.normal(key, (TOKENS, width), jnp.float32), -8.0, 8.0)
    return base.astype(jnp.bfloat16)


def set_ends(array, key, least, high):
    spot = [jax.random.randint(jax.random.fold_in(key, axis), (), 0, length) for axis, length in enumerate(array.shape)]
    longest = array.shape.index(max(array.shape))
    neighbour = spot[:longest] + [(spot[longest] + 1) % array.shape[longest]] + spot[longest + 1:]
    return array.at[tuple(spot)].set(least).at[tuple(neighbour)].set(high)


def steps_of(stream_key, extent, pieces, smallest, high):
    level = 1.0
    for axis_at, shards_of in pieces:
        steps = jax.random.uniform(jax.random.fold_in(jax.random.fold_in(stream_key, 6), axis_at), (shards_of,), jnp.float32, smallest / len(pieces), high / len(pieces))
        level = level * jnp.repeat(jnp.exp(steps), extent[axis_at] // shards_of).reshape((-1,) + (1,) * (len(extent) - 1 - axis_at))
    return level


def scatter_about(stream_key, shape, scale, limit, cuts=(), kind=jnp.bfloat16):
    factor_of = steps_of(stream_key, shape, cuts, -0.22, 0.18) if cuts else 1.0
    result = jax.random.normal(stream_key, shape, jnp.float32) * scale * factor_of
    return jnp.minimum(jnp.maximum(result, -limit), limit).astype(kind)


def setup_inputs(seed: int = 0) -> dict:
    arg_keys = jax.random.split(jax.random.key(seed), 11)
    hidden = draw_hidden(jax.random.fold_in(arg_keys[10], 71), 0)
    queries = draw_queries(jax.random.fold_in(arg_keys[10], 71), 0)
    new_cache = draw_new_cache(jax.random.fold_in(arg_keys[10], 71), 0)
    cache_pool = scatter_about(arg_keys[3], (DEVICES * POOL_DEV, PAGE, 2 * HD), 1.0, 6.0, ((0, 32),))
    cache_length = set_ends(jax.random.randint(arg_keys[4], (REQUESTS,), 1, CACHE_MAX + 1), jax.random.fold_in(arg_keys[4], 1), 1, CACHE_MAX).astype(jnp.int32)
    page_table = draw_page_table(jax.random.fold_in(arg_keys[10], 71), 0)
    send_map = draw_send_map(jax.random.fold_in(arg_keys[10], 71), 0)
    out_weight = scatter_about(arg_keys[7], (HEADS * HD, D), HD ** -0.5, 0.5)
    norm_gain = jnp.clip(1.0 + 0.18 * jax.random.normal(arg_keys[8], (D,), jnp.float32), 0.099609375, 1.8984375).astype(jnp.bfloat16)
    ffn_weight = scatter_about(arg_keys[9], (3, D, FF), D ** -0.5, 0.15625, ((2, 4),))
    return dict(hidden=hidden, queries=queries, new_cache=new_cache, cache_pool=cache_pool, cache_length=cache_length, page_table=page_table, send_map=send_map, out_weight=out_weight, norm_gain=norm_gain, ffn_weight=ffn_weight)


masked_score = -1e+30

def visibility(lengths, first_page, page_size, window, new_count, cache_slots):
    query_pos = lengths[:, None] + jnp.arange(new_count, dtype=jnp.int32)[None, :]
    cache_pos = first_page[:, None] * page_size + jnp.arange(cache_slots, dtype=jnp.int32)[None, :]
    cache_seen = (cache_pos[:, None, :] < lengths[:, None, None]) & (cache_pos[:, None, :] > query_pos[:, :, None] - window)
    offsets = jnp.arange(new_count, dtype=jnp.int32)
    fresh_seen = offsets[None, None, :] <= offsets[None, :, None]
    fresh_seen = jnp.broadcast_to(fresh_seen, (lengths.shape[0], new_count, new_count))
    return jnp.concatenate([cache_seen, fresh_seen], axis=2)

def normalize(scores, seen):
    scores = jnp.where(seen[:, None], scores, masked_score)
    top_score = lax.optimization_barrier(jnp.max(scores, axis=-1, keepdims=True))
    weights = jnp.where(seen[:, None], jnp.exp(scores - top_score), 0.0)
    return (weights / lax.optimization_barrier(jnp.sum(weights, axis=-1, keepdims=True))).astype(jnp.bfloat16)

def feed_forward(middle, norm_gain, ffn_weight):
    middle_f = middle.astype(jnp.float32)
    scale_rows = lax.rsqrt(lax.optimization_barrier(jnp.mean(middle_f * middle_f, axis=-1, keepdims=True)) + 1e-06)
    normed = (middle_f * scale_rows * norm_gain.astype(jnp.float32)).astype(jnp.bfloat16)
    gate_part = jnp.dot(normed, ffn_weight[0], preferred_element_type=jnp.float32)
    up_part = jnp.dot(normed, ffn_weight[1], preferred_element_type=jnp.float32)
    activated = (jax.nn.gelu(gate_part, approximate=True) * up_part).astype(jnp.bfloat16)
    ffn_sum = lax.dot_general(activated, ffn_weight[2], (((1,), (1,)), ((), ())), preferred_element_type=jnp.float32)
    return (middle_f + ffn_sum).astype(jnp.bfloat16)

def reference(hidden, queries, new_cache, cache_pool, cache_length, page_table, send_map, out_weight, norm_gain, ffn_weight):
    cache_slots = WPAGES * PAGE

    def one_device(inputs):
        device, hidden_rows, query_rows, fresh_rows, lengths, table = inputs
        source = table // CAP
        slot_index = table % CAP
        pool_index = (source * POOL_DEV + send_map[source, device * CAP + slot_index]).astype(jnp.int32)
        window_rows = cache_pool[pool_index].reshape(REQ_DEV, cache_slots, 2 * HD)
        both = jnp.concatenate([window_rows, fresh_rows.reshape(REQ_DEV, NEW, 2 * HD)], axis=1)
        key_rows = both[:, :, :HD].astype(jnp.float32)
        value_rows = both[:, :, HD:].astype(jnp.float32)
        first_page = jnp.maximum(lengths - W + 1, 0) // PAGE
        seen = visibility(lengths, first_page, PAGE, W, NEW, cache_slots)
        query_block = query_rows.reshape(REQ_DEV, NEW, HEADS, HD).astype(jnp.float32)
        scores = jnp.einsum('rnhe,rke->rhnk', query_block, key_rows) / math.sqrt(HD)
        attn_probs = normalize(scores, seen)
        attended = jnp.einsum('rhnk,rke->rnhe', attn_probs.astype(jnp.float32), value_rows)
        attended = attended.astype(jnp.bfloat16).reshape(TOK_DEV, HEADS * HD)
        projected = jnp.dot(attended, out_weight, preferred_element_type=jnp.float32)
        middle = (hidden_rows.astype(jnp.float32) + projected).astype(jnp.bfloat16)
        return feed_forward(middle, norm_gain, ffn_weight)
    outputs = lax.map(one_device, (jnp.arange(DEVICES, dtype=jnp.int32), hidden.reshape(DEVICES, TOK_DEV, D), queries.reshape(DEVICES, TOK_DEV, HEADS * HD), new_cache.reshape(DEVICES, TOK_DEV, 2 * HD), cache_length.reshape(DEVICES, REQ_DEV), page_table.reshape(DEVICES, REQ_DEV, WPAGES)))
    return outputs.reshape(TOKENS, D)
```

```python
import functools
import math

import jax
import jax.numpy as jnp
from jax import lax
from jax.experimental import pallas as pl
from jax.experimental.pallas import tpu as pltpu
from jax.sharding import PartitionSpec as P

W = 1024
PAGE = 64
HALVES = 2
NT = (((1,), (1,)), ((), ()))
MESH = pl.DeviceIdType.MESH


def layer_kernel(
    lengths_ref, table_ref, arrived_ref, hidden_ref, queries_ref, new_ref, gain_ref, ow_hbm, fw_hbm,
    out_ref,
    ow, fw, kv, att, middle, loc, rem, own_part,
    send_pair, send_fold, send_far, got_pair, got_fold, got_far,
    w_sem, ssem, rsem,
):
    requests, wpages = table_ref.shape
    page = arrived_ref.shape[1]
    pair_width = arrived_ref.shape[2]
    hd = pair_width // 2
    tok, width = queries_ref.shape
    heads = width // hd
    new = tok // requests
    cached = wpages * page
    keys = cached + new
    per_half = requests // HALVES
    rows = tok // HALVES
    ff = fw.shape[2]
    group = 4
    for_heads = 4

    me_r = lax.axis_index("req")
    g = lax.axis_index("grp")
    hi, lo = g // 2, lax.rem(g, 2)
    partner = (me_r, hi * 2 + (1 - lo))
    peer = (me_r, (1 - hi) * 2 + lo)

    ow_copy = pltpu.make_async_copy(ow_hbm, ow, w_sem.at[0])
    ow_copy.start()
    fw_copies = [pltpu.make_async_copy(fw_hbm.at[k], fw.at[k], w_sem.at[k + 1]) for k in range(3)]
    for copy in fw_copies:
        copy.start()

    barrier = pltpu.get_barrier_semaphore()
    for other in (partner, peer):
        pl.semaphore_signal(barrier, inc=1, device_id=other, device_id_type=MESH)
    pl.semaphore_wait(barrier, 2)

    def remote(src, dst, slot, where):
        return pltpu.make_async_remote_copy(
            src_ref=src, dst_ref=dst, send_sem=ssem.at[slot], recv_sem=rsem.at[slot],
            device_id=where, device_id_type=MESH,
        )

    to_partner = [remote(loc.at[c, 0], loc.at[c, 1], c, partner) for c in range(HALVES)]
    to_peer = [remote(loc.at[c, 0], rem.at[c, 0], 2 + c, peer) for c in range(HALVES)]
    forward = [remote(rem.at[c, 0], rem.at[c, 1], 4 + c, partner) for c in range(HALVES)]
    pair_sum = [remote(send_pair.at[c], got_pair.at[c], 6 + c, partner) for c in range(HALVES)]
    fold_sum = [remote(send_fold.at[c], got_fold.at[c], 8 + c, partner) for c in range(HALVES)]
    far_sum = [remote(send_far.at[c], got_far.at[c], 10 + c, peer) for c in range(HALVES)]

    scale = math.log2(math.e) / math.sqrt(hd)

    for c in range(HALVES):

        def attend(t, carry):
            r = c * per_half + t
            for j in range(wpages):
                kv[j * page:(j + 1) * page, :] = arrived_ref[table_ref[r, j]]
            kv[cached:keys, :] = new_ref[pl.ds(pl.multiple_of(r * new, new), new), :]
            length = lengths_ref[r]
            first = jnp.maximum(length - W + 1, 0) // PAGE * page
            col = lax.broadcasted_iota(jnp.int32, (new, keys), 1)
            row = lax.broadcasted_iota(jnp.int32, (new, keys), 0)
            pos = jnp.where(col < cached, col + first, col - cached + length)
            top = jnp.where(col < cached, length - 1, row + length)
            seen = (pos <= top) & (pos > row + length - W)
            bias = jnp.where(seen, 0.0, -1e30).astype(jnp.float32)
            for h0 in range(0, heads, for_heads):
                hs = range(h0, min(h0 + for_heads, heads))
                q = jnp.concatenate(
                    [queries_ref[pl.ds(pl.multiple_of(r * new, new), new), h * hd:(h + 1) * hd] for h in hs], axis=0
                )
                s = lax.dot_general(q, kv[:, :hd], NT, preferred_element_type=jnp.float32)
                s = s.reshape(len(hs), new, keys) * scale + bias[None]
                top_score = jnp.max(s, axis=-1, keepdims=True)
                p = jnp.exp2(s - top_score)
                total = jnp.sum(p, axis=-1, keepdims=True)
                p = p.astype(jnp.bfloat16).reshape(len(hs) * new, keys)
                o = jnp.dot(p, kv[:, hd:], preferred_element_type=jnp.float32)
                o = (o.reshape(len(hs), new, hd) / total).astype(jnp.bfloat16)
                for i, h in enumerate(hs):
                    att[pl.ds(pl.multiple_of(t * new, new), new), h * hd:(h + 1) * hd] = o[i]
            return carry

        lax.fori_loop(0, per_half, attend, 0)
        if c == 0:
            ow_copy.wait()
        projected = jnp.dot(att[...], ow[...], preferred_element_type=jnp.float32)
        mid = (hidden_ref[c * rows:(c + 1) * rows, :].astype(jnp.float32) + projected).astype(jnp.bfloat16)
        middle[c * rows:(c + 1) * rows, :] = mid
        mid_f = mid.astype(jnp.float32)
        rs = lax.rsqrt(jnp.mean(mid_f * mid_f, axis=-1, keepdims=True) + 1e-06)
        loc[c, 0] = (mid_f * rs * gain_ref[...].astype(jnp.float32)).astype(jnp.bfloat16)
        to_peer[c].start()
        to_partner[c].start()

    cols = [(a, min(a + 512, ff)) for a in range(0, ff, 512)]

    def ffn(x):
        parts = []
        for a, b in cols:
            gate = jnp.dot(x, fw[0, :, a:b], preferred_element_type=jnp.float32)
            up = jnp.dot(x, fw[1, :, a:b], preferred_element_type=jnp.float32)
            parts.append((jax.nn.gelu(gate, approximate=True) * up).astype(jnp.bfloat16))
        act = jnp.concatenate(parts, axis=1)
        return lax.dot_general(act, fw[2], NT, preferred_element_type=jnp.float32)

    for copy in fw_copies:
        copy.wait()

    def local(c):
        to_partner[c].wait_recv()
        part = ffn(loc[c].reshape(2 * rows, width))
        own_part[c] = part[:rows]
        send_pair[c] = part[rows:].astype(jnp.bfloat16)
        pair_sum[c].start()

    def far(c):
        forward[c].wait_recv()
        part = ffn(rem[c].reshape(2 * rows, width))
        send_fold[c] = part[rows:].astype(jnp.bfloat16)
        fold_sum[c].start()
        return part[:rows]

    def fold(c, part):
        fold_sum[c].wait_recv()
        send_far[c] = (part + got_fold[c].astype(jnp.float32)).astype(jnp.bfloat16)
        far_sum[c].start()

    def finish(c):
        pair_sum[c].wait_recv()
        own = own_part[c] + middle[c * rows:(c + 1) * rows, :].astype(jnp.float32) + got_pair[c].astype(jnp.float32)
        far_sum[c].wait_recv()
        out_ref[c * rows:(c + 1) * rows, :] = (own + got_far[c].astype(jnp.float32)).astype(jnp.bfloat16)

    local(0)
    to_peer[0].wait_recv()
    forward[0].start()
    local(1)
    part = far(0)
    to_peer[1].wait_recv()
    forward[1].start()
    fold(0, part)
    part = far(1)
    fold(1, part)
    finish(0)
    finish(1)
    for copies in (to_partner, to_peer, forward, pair_sum, fold_sum, far_sum):
        for copy in copies:
            copy.wait_send()


def layer(lengths, table, arrived, hidden, queries, new_cache, gain, out_weight, ffn_weight):
    tok, width = queries.shape
    requests, wpages = table.shape
    page, pair_width = arrived.shape[1:]
    new = tok // requests
    rows = tok // HALVES
    bf, f32 = jnp.bfloat16, jnp.float32
    vm = pl.BlockSpec(memory_space=pltpu.VMEM)
    sm = pl.BlockSpec(memory_space=pltpu.SMEM)
    anyspace = pl.BlockSpec(memory_space=pl.ANY)
    half = (HALVES, rows, width)
    return pl.pallas_call(
        layer_kernel,
        out_shape=jax.ShapeDtypeStruct((tok, width), bf),
        in_specs=[sm, sm, vm, vm, vm, vm, vm, anyspace, anyspace],
        out_specs=vm,
        scratch_shapes=[
            pltpu.VMEM(out_weight.shape, bf),
            pltpu.VMEM(ffn_weight.shape, bf),
            pltpu.VMEM((wpages * page + new, pair_width), bf),
            pltpu.VMEM((rows, width), bf),
            pltpu.VMEM((tok, width), bf),
            pltpu.VMEM((HALVES, 2, rows, width), bf),
            pltpu.VMEM((HALVES, 2, rows, width), bf),
            pltpu.VMEM(half, f32),
        ] + [pltpu.VMEM(half, bf)] * 6 + [
            pltpu.SemaphoreType.DMA((4,)),
            pltpu.SemaphoreType.DMA((12,)),
            pltpu.SemaphoreType.DMA((12,)),
        ],
        compiler_params=pltpu.CompilerParams(
            collective_id=1, has_side_effects=True, vmem_limit_bytes=56 * 2**20
        ),
        name="layer",
    )(lengths, table, arrived, hidden, queries, new_cache, gain.reshape(1, -1), out_weight, ffn_weight)


def per_device(
    hidden,
    queries,
    new_cache,
    cache_pool,
    cache_length,
    page_table,
    send_map,
    out_weight,
    norm_gain,
    ffn_weight,
):
    outgoing = cache_pool[send_map[0]]
    arrived = lax.all_to_all(outgoing, ("req", "grp"), split_axis=0, concat_axis=0, tiled=True)
    return layer(
        cache_length, page_table, arrived, hidden, queries, new_cache, norm_gain, out_weight, ffn_weight
    )


def solution(mesh):
    return jax.shard_map(
        per_device,
        mesh=mesh,
        in_specs=(
            P(("req", "grp"), None),
            P(("req", "grp"), None),
            P(("req", "grp"), None),
            P(("req", "grp"), None, None),
            P(("req", "grp")),
            P(("req", "grp"), None),
            P(("req", "grp"), None),
            P(),
            P(),
            P(None, None, "grp"),
        ),
        out_specs=P(("req", "grp"), None),
        check_vma=False,
    )
```

```python
import functools
import math

import jax
import jax.numpy as jnp
from jax import lax
from jax.experimental import pallas as pl
from jax.experimental.pallas import tpu as pltpu
from jax.sharding import PartitionSpec as P

W = 1024
PAGE = 64
HALVES = 2
NT = (((1,), (1,)), ((), ()))
MESH = pl.DeviceIdType.MESH


def layer_kernel(
    lengths_ref, table_ref, arrived_ref, hidden_ref, queries_ref, new_ref, gain_ref, ow_hbm, fw_hbm,
    out_ref,
    ow, fw, kv, att, middle, loc, rem, own_part,
    send_pair, send_fold, send_far, got_pair, got_fold, got_far,
    w_sem, ssem, rsem,
):
    requests, wpages = table_ref.shape
    page = arrived_ref.shape[1]
    pair_width = arrived_ref.shape[2]
    hd = pair_width // 2
    tok, width = queries_ref.shape
    heads = width // hd
    new = tok // requests
    cached = wpages * page
    keys = cached + new
    per_half = requests // HALVES
    rows = tok // HALVES
    ff = fw.shape[2]
    for_heads = 6

    me_r = lax.axis_index("req")
    g = lax.axis_index("grp")
    hi, lo = g // 2, lax.rem(g, 2)
    partner = (me_r, hi * 2 + (1 - lo))
    peer = (me_r, (1 - hi) * 2 + lo)

    ow_copy = pltpu.make_async_copy(ow_hbm, ow, w_sem.at[0])
    ow_copy.start()
    fw_copies = [pltpu.make_async_copy(fw_hbm.at[k], fw.at[k], w_sem.at[k + 1]) for k in range(3)]
    for copy in fw_copies:
        copy.start()

    barrier = pltpu.get_barrier_semaphore()
    for other in (partner, peer):
        pl.semaphore_signal(barrier, inc=1, device_id=other, device_id_type=MESH)
    pl.semaphore_wait(barrier, 2)

    def remote(src, dst, slot, where):
        return pltpu.make_async_remote_copy(
            src_ref=src, dst_ref=dst, send_sem=ssem.at[slot], recv_sem=rsem.at[slot],
            device_id=where, device_id_type=MESH,
        )

    def piece(r, side, where):
        c, t = r // per_half, lax.rem(r, per_half)
        at = pl.ds(pl.multiple_of(t * new, new), new)
        if side == 0:
            return remote(loc.at[c, 0, at], loc.at[c, 1, at], r, where)
        return remote(loc.at[c, 0, at], rem.at[c, 0, at], requests + r, where)

    def to_partner(r):
        return piece(r, 0, partner)

    def to_peer(r):
        return piece(r, 1, peer)

    base = 2 * requests
    forward = [remote(rem.at[c, 0], rem.at[c, 1], base + 0 + c, partner) for c in range(HALVES)]
    pair_sum = [remote(send_pair.at[c], got_pair.at[c], base + 2 + c, partner) for c in range(HALVES)]
    fold_sum = [remote(send_fold.at[c], got_fold.at[c], base + 4 + c, partner) for c in range(HALVES)]
    far_sum = [remote(send_far.at[c], got_far.at[c], base + 6 + c, peer) for c in range(HALVES)]

    scale = math.log2(math.e) / math.sqrt(hd)

    def attend(r, carry):
        for j in range(wpages):
            kv[j * page:(j + 1) * page, :] = arrived_ref[table_ref[r, j]]
        here = pl.ds(pl.multiple_of(r * new, new), new)
        kv[cached:keys, :] = new_ref[here, :]
        length = lengths_ref[r]
        first = jnp.maximum(length - W + 1, 0) // PAGE * page
        col = lax.broadcasted_iota(jnp.int32, (new, keys), 1)
        row = lax.broadcasted_iota(jnp.int32, (new, keys), 0)
        pos = jnp.where(col < cached, col + first, col - cached + length)
        top = jnp.where(col < cached, length - 1, row + length)
        seen = (pos <= top) & (pos > row + length - W)
        bias = jnp.where(seen, 0.0, -1e30).astype(jnp.float32)
        for h0 in range(0, heads, for_heads):
            hs = range(h0, min(h0 + for_heads, heads))
            q = jnp.concatenate([queries_ref[here, h * hd:(h + 1) * hd] for h in hs], axis=0)
            s = lax.dot_general(q, kv[:, :hd], NT, preferred_element_type=jnp.float32)
            s = s.reshape(len(hs), new, keys) * scale + bias[None]
            top_score = jnp.max(s, axis=-1, keepdims=True)
            p = jnp.exp2(s - top_score)
            total = jnp.sum(p, axis=-1, keepdims=True)
            p = p.astype(jnp.bfloat16).reshape(len(hs) * new, keys)
            o = jnp.dot(p, kv[:, hd:], preferred_element_type=jnp.float32)
            o = (o.reshape(len(hs), new, hd) / total).astype(jnp.bfloat16)
            for i, h in enumerate(hs):
                att[:, h * hd:(h + 1) * hd] = o[i]

        @pl.when(r == 0)
        def _():
            ow_copy.wait()

        projected = jnp.dot(att[...], ow[...], preferred_element_type=jnp.float32)
        mid = (hidden_ref[here, :].astype(jnp.float32) + projected).astype(jnp.bfloat16)
        middle[here, :] = mid
        mid_f = mid.astype(jnp.float32)
        rs = lax.rsqrt(jnp.mean(mid_f * mid_f, axis=-1, keepdims=True) + 1e-06)
        normed = (mid_f * rs * gain_ref[...].astype(jnp.float32)).astype(jnp.bfloat16)
        loc[r // per_half, 0, pl.ds(pl.multiple_of(lax.rem(r, per_half) * new, new), new), :] = normed
        to_peer(r).start()
        to_partner(r).start()
        return carry

    lax.fori_loop(0, requests, attend, 0)

    cols = [(a, min(a + 512, ff)) for a in range(0, ff, 512)]

    def ffn(x):
        parts = []
        for a, b in cols:
            gate = jnp.dot(x, fw[0, :, a:b], preferred_element_type=jnp.float32)
            up = jnp.dot(x, fw[1, :, a:b], preferred_element_type=jnp.float32)
            parts.append((jax.nn.gelu(gate, approximate=True) * up).astype(jnp.bfloat16))
        act = jnp.concatenate(parts, axis=1)
        return lax.dot_general(act, fw[2], NT, preferred_element_type=jnp.float32)

    for copy in fw_copies:
        copy.wait()

    def local(c):
        for t in range(per_half):
            to_partner(c * per_half + t).wait_recv()
        part = ffn(loc[c].reshape(2 * rows, width))
        own_part[c] = part[:rows]
        send_pair[c] = part[rows:].astype(jnp.bfloat16)
        pair_sum[c].start()

    def far(c):
        forward[c].wait_recv()
        part = ffn(rem[c].reshape(2 * rows, width))
        send_fold[c] = part[rows:].astype(jnp.bfloat16)
        fold_sum[c].start()
        return part[:rows]

    def fold(c, part):
        fold_sum[c].wait_recv()
        send_far[c] = (part + got_fold[c].astype(jnp.float32)).astype(jnp.bfloat16)
        far_sum[c].start()

    def finish(c):
        pair_sum[c].wait_recv()
        own = own_part[c] + middle[c * rows:(c + 1) * rows, :].astype(jnp.float32) + got_pair[c].astype(jnp.float32)
        far_sum[c].wait_recv()
        out_ref[c * rows:(c + 1) * rows, :] = (own + got_far[c].astype(jnp.float32)).astype(jnp.bfloat16)

    def pass_on(c):
        for t in range(per_half):
            to_peer(c * per_half + t).wait_recv()
        forward[c].start()

    local(0)
    pass_on(0)
    local(1)
    part = far(0)
    pass_on(1)
    fold(0, part)
    part = far(1)
    fold(1, part)
    finish(0)
    finish(1)
    for r in range(requests):
        to_partner(r).wait_send()
        to_peer(r).wait_send()
    for copies in (forward, pair_sum, fold_sum, far_sum):
        for copy in copies:
            copy.wait_send()


def layer(lengths, table, arrived, hidden, queries, new_cache, gain, out_weight, ffn_weight):
    tok, width = queries.shape
    requests, wpages = table.shape
    page, pair_width = arrived.shape[1:]
    new = tok // requests
    rows = tok // HALVES
    bf, f32 = jnp.bfloat16, jnp.float32
    vm = pl.BlockSpec(memory_space=pltpu.VMEM)
    sm = pl.BlockSpec(memory_space=pltpu.SMEM)
    anyspace = pl.BlockSpec(memory_space=pl.ANY)
    half = (HALVES, rows, width)
    return pl.pallas_call(
        layer_kernel,
        out_shape=jax.ShapeDtypeStruct((tok, width), bf),
        in_specs=[sm, sm, vm, vm, vm, vm, vm, anyspace, anyspace],
        out_specs=vm,
        scratch_shapes=[
            pltpu.VMEM(out_weight.shape, bf),
            pltpu.VMEM(ffn_weight.shape, bf),
            pltpu.VMEM((wpages * page + new, pair_width), bf),
            pltpu.VMEM((new, width), bf),
            pltpu.VMEM((tok, width), bf),
            pltpu.VMEM((HALVES, 2, rows, width), bf),
            pltpu.VMEM((HALVES, 2, rows, width), bf),
            pltpu.VMEM(half, f32),
        ] + [pltpu.VMEM(half, bf)] * 6 + [
            pltpu.SemaphoreType.DMA((4,)),
            pltpu.SemaphoreType.DMA((2 * requests + 4 * HALVES,)),
            pltpu.SemaphoreType.DMA((2 * requests + 4 * HALVES,)),
        ],
        compiler_params=pltpu.CompilerParams(
            collective_id=1, has_side_effects=True, vmem_limit_bytes=56 * 2**20
        ),
        name="layer",
    )(lengths, table, arrived, hidden, queries, new_cache, gain.reshape(1, -1), out_weight, ffn_weight)


def exchange_kernel(map_ref, pool_hbm, out_ref, pool, outgoing, pool_sem, ssem, rsem, *, n, groups):
    cap = map_ref.shape[1] // n
    me_r = lax.axis_index("req")
    me_g = lax.axis_index("grp")
    me = me_r * groups + me_g
    load = pltpu.make_async_copy(pool_hbm, pool, pool_sem)
    load.start()

    barrier = pltpu.get_barrier_semaphore()

    def greet(k, carry):
        other = lax.rem(me + k, n)
        pl.semaphore_signal(
            barrier, inc=1, device_id=(other // groups, lax.rem(other, groups)), device_id_type=MESH
        )
        return carry

    lax.fori_loop(1, n, greet, 0)
    load.wait()
    pl.semaphore_wait(barrier, n - 1)

    def copy_of(k, source, target, held_by):
        return pltpu.make_async_remote_copy(
            src_ref=outgoing.at[pl.ds(source * cap, cap)],
            dst_ref=out_ref.at[pl.ds(target * cap, cap)],
            send_sem=ssem.at[k], recv_sem=rsem.at[k],
            device_id=(held_by // groups, lax.rem(held_by, groups)), device_id_type=MESH,
        )

    def send(i, carry):
        odd = lax.rem(i, 2)
        k = n // 2 + (2 * odd - 1) * ((i + 1) // 2)
        other = lax.rem(me + k, n)
        for c in range(cap):
            outgoing[other * cap + c] = pool[map_ref[0, other * cap + c]]
        copy_of(k, other, me, other).start()
        return carry

    lax.fori_loop(0, n - 1, send, 0)
    for c in range(cap):
        out_ref[me * cap + c] = pool[map_ref[0, me * cap + c]]

    def receive(k, carry):
        other = lax.rem(me + k, n)
        source = lax.rem(me + n - k, n)
        copy_of(k, other, source, other).wait()
        return carry

    lax.fori_loop(1, n, receive, 0)


def exchange(pool, send_map, n, groups):
    slots = send_map.shape[1]
    page = pool.shape[1:]
    return pl.pallas_call(
        functools.partial(exchange_kernel, n=n, groups=groups),
        out_shape=jax.ShapeDtypeStruct((slots,) + page, pool.dtype),
        in_specs=[pl.BlockSpec(memory_space=pltpu.SMEM), pl.BlockSpec(memory_space=pl.ANY)],
        out_specs=pl.BlockSpec(memory_space=pltpu.VMEM),
        scratch_shapes=[
            pltpu.VMEM(pool.shape, pool.dtype),
            pltpu.VMEM((slots,) + page, pool.dtype),
            pltpu.SemaphoreType.DMA,
            pltpu.SemaphoreType.DMA((n,)),
            pltpu.SemaphoreType.DMA((n,)),
        ],
        compiler_params=pltpu.CompilerParams(
            collective_id=0, has_side_effects=True, vmem_limit_bytes=56 * 2**20
        ),
        name="exchange",
    )(send_map, pool)


def per_device(
    groups,
    n,
    hidden,
    queries,
    new_cache,
    cache_pool,
    cache_length,
    page_table,
    send_map,
    out_weight,
    norm_gain,
    ffn_weight,
):
    arrived = exchange(cache_pool, send_map, n, groups)
    return layer(
        cache_length, page_table, arrived, hidden, queries, new_cache, norm_gain, out_weight, ffn_weight
    )


def solution(mesh):
    return jax.shard_map(
        functools.partial(per_device, mesh.shape["grp"], mesh.size),
        mesh=mesh,
        in_specs=(
            P(("req", "grp"), None),
            P(("req", "grp"), None),
            P(("req", "grp"), None),
            P(("req", "grp"), None, None),
            P(("req", "grp")),
            P(("req", "grp"), None),
            P(("req", "grp"), None),
            P(),
            P(),
            P(None, None, "grp"),
        ),
        out_specs=P(("req", "grp"), None),
        check_vma=False,
    )
```
